128 devices in a mesh: grp: 8 (over z_hi, x), sub: 16 (over y, z_lo, core).
Axes of the slice: x: 4, y: 4, z: 4 (z_hi: 2, z_lo: 2; z = z_hi * 2 + z_lo), core: 2. Of those that a mesh axis runs over, the one named last changes fastest.
Arguments:
- bem_tiles: float32 [16384, 16384], P('grp', 'sub'), may hold values from -0.03125 to 0.03125
- leaf_inverse: float32 [8, 32, 1024, 1024], P('grp', 'sub'), may hold values from -1.5 to 1.5
- coupling: float32 [8, 32, 1024, 512], P('grp', 'sub'), may hold values from -0.0625 to 0.0625
- schur_inverse: float32 [8, 512, 512], P('grp', None, 'sub'), may hold values from -1.5 to 1.5
- leaf_load: float32 [8, 32, 1024, 128], P('grp', 'sub'), may hold values from -6 to 6
- sep_load: float32 [8, 512, 128], P('grp'), may hold values from -6 to 6
- surf_load: float32 [16384, 128], P(('grp', 'sub')), may hold values from -6 to 6
- surf_start: float32 [16384, 128], P(('grp', 'sub')), may hold values from -6 to 6
- flux_weight: float32 [8, 32, 8, 128], P('grp', 'sub'), may hold values from 0.25 to 1
- trace_weight: float32 [8, 32, 8, 128], P('grp', 'sub'), may hold values from 0.25 to 1
- leaf_sizes: int32 [8, 32], P('grp', 'sub'), may hold values from 512 to 1024
- block_counts: int32 [8, 32], P('grp', 'sub'), may hold values from 4 to 8
- block_owner: int32 [8, 32, 8, 1], P('grp', 'sub'), may hold values from 0 to 15; in each aligned block of 16 rows (0 to 15, 16 to 31, ..., all dimensions but the last counted through in order) at most 2 rows name the same one
Outputs:
- solution: float32 [8, 32, 1024, 128], P('grp', 'sub')
- sep_value: float32 [8, 512, 128], P('grp', 'sub')
- pressure: float32 [16384, 128], P(('grp', 'sub'))
The draws below stay inside these ranges and needn't reach their ends.
Inputs may be any that keep to these rules, and one draw needn't show every extreme that they name: `block_owner`: of the 16 entries of one device, live or not, at most 2 name the same owner, and some device has 2 entries naming one owner.
All inputs are finite; a program needn't handle non-finite values.
Results may differ from the reference program's by a relative error of at most 0.00018.
Values sent between devices are 32-bit elements; how exact they have to be, the bound alone decides.
No kernel may reach another device: no remote copies, remote signals or barrier semaphores. Data moves between devices by JAX's collectives and lax.ppermute only.
A program may use at most 128 MiB of HBM per device.

```python
import math
import jax
import jax.numpy as jnp
import numpy as np
from jax import lax

LEAF = 1024
SEP = 512
SURF_DEV = 128
SUB_DEV = 2
CAP = 2
SWEEPS = 3
LOADS = 128
GROUPS = 8
NSUBD = 32
NS = 16384
MAXB = 8
N_SUB = 16


def draw_leaf_inverse(key, part):
    first, second = jax.random.split(jax.random.fold_in(key, 11))
    spread = jax.random.normal(first, (GROUPS, NSUBD, LEAF, LEAF), jnp.float32) * (0.3 / math.sqrt(LEAF))
    diagonal = jax.random.uniform(second, (GROUPS, NSUBD, LEAF), jnp.float32, 0.4, 0.7)
    return spread + diagonal[..., None] * jnp.eye(LEAF, dtype=jnp.float32)


def draw_schur_inverse(key, part):
    first, second = jax.random.split(jax.random.fold_in(key, 23))
    spread = jax.random.normal(first, (GROUPS, SEP, SEP), jnp.float32) * (0.3 / math.sqrt(SEP))
    diagonal = jax.random.uniform(second, (GROUPS, SEP), jnp.float32, 0.4, 0.7)
    return spread + diagonal[..., None] * jnp.eye(SEP, dtype=jnp.float32)


def with_ends(result, own_key, low, largest):
    index_at = [jax.random.randint(jax.random.fold_in(own_key, axis), (), 0, length) for axis, length in enumerate(result.shape)]
    longest = result.shape.index(max(result.shape))
    beside = index_at[:longest] + [(index_at[longest] + 1) % result.shape[longest]] + index_at[longest + 1:]
    return result.at[tuple(index_at)].set(low).at[tuple(beside)].set(largest)


def spiked(array, rng, source, target, parts, factor):
    owner, partner = [(jnp.arange(array.shape[axis_at]) // (array.shape[axis_at] // parts)).reshape([-1 if axis == axis_at else 1 for axis in range(array.ndim)]) for axis_at in (source, target)]
    chosen = jax.random.permutation(rng, parts)[partner]
    strong = (owner == chosen) | (owner == (partner + parts // 2) % parts)
    return jnp.where(strong, factor * array, array)


def block_levels(own_key, dims, pieces, least, top_value):
    level = 1.0
    for axis_at, blocks in pieces:
        steps = jax.random.uniform(jax.random.fold_in(jax.random.fold_in(own_key, 6), axis_at), (blocks,), jnp.float32, least / len(pieces), top_value / len(pieces))
        level = level * jnp.repeat(jnp.exp(steps), dims[axis_at] // blocks).reshape((-1,) + (1,) * (len(dims) - 1 - axis_at))
    return level


def deal_out(own_key, own, number, rows, count, top, reach, lean):
    ranking = jax.random.permutation(own_key, count)
    crowded, usual = load_shares(count, rows * top, reach, lean, True), load_shares(count, rows * top, reach, lean, False)
    places = jnp.arange(count)

    def named(lengths, turn):
        used = int((lengths > 0).sum())
        fixed = max(1, used // 4)
        shifted = fixed + (places - fixed + turn * (used - fixed)) % max(1, count - fixed)
        return jnp.zeros((count,), jnp.int32).at[ranking[jnp.where(places < fixed, places, shifted)]].set(jnp.asarray(lengths, jnp.int32))

    lengths = jnp.where(number % 4 == 0, named(crowded, number // 4), named(usual, number - number // 4 - 1))
    mixed = jax.random.permutation(jax.random.fold_in(own, 3), count)
    source_of, taker = mixed[0:count // 2 * 2:2], mixed[1:count // 2 * 2:2]
    margin = jnp.minimum(lengths[source_of] - 1, reach - lengths[taker]) // 2
    margin = jnp.where((source_of == ranking[0]) | (taker == ranking[0]) | (lengths[taker] == 0), 0, jnp.maximum(margin, 0))
    shifted = jax.random.randint(jax.random.fold_in(own, 4), (count // 2,), 0, 1 << 20) % (margin + 1)
    lengths = lengths.at[source_of].add(-shifted).at[taker].add(shifted)
    items = jnp.searchsorted(jnp.cumsum(lengths), jnp.arange(rows * top), side="right").astype(jnp.int32)
    listing = items.reshape(top, rows).T
    listing = listing[jax.random.permutation(jax.random.fold_in(own, 1), rows)]
    turn = jax.random.randint(jax.random.fold_in(own, 2), (rows, 1), 0, top)
    return jnp.take_along_axis(listing, (jnp.arange(top)[None, :] + turn) % top, axis=1)


def load_shares(number_of, total, reach, skew, full):
    portions = [(1 << 20) // math.isqrt(grade ** skew) + 1 for grade in range(1, number_of + 1)]
    largest = reach if full else min(reach, max(-(-total // number_of), total * portions[0] // sum(portions)))
    least = 1 if total - largest >= number_of - 1 else 0
    given, surplus = [largest] + [least] * (number_of - 1), total - largest - least * (number_of - 1)
    while surplus > 0:
        movable = [i for i in range(1, number_of) if given[i] < largest] or [i for i in range(1, number_of) if given[i] < reach]
        mass, budget = sum([portions[i] for i in movable]), surplus
        for i in movable:
            addition = min(reach - given[i], max(1, budget * portions[i] // mass), surplus)
            given[i] = given[i] + addition
            surplus = surplus - addition
    return np.array(given)


def gaussian(own_key, shape, deviation, limit, cuts=(), held_as=jnp.bfloat16):
    array = deviation * jax.random.normal(own_key, shape, jnp.float32)
    if cuts:
        array = array * block_levels(own_key, shape, cuts, -0.22, 0.18)
    return jnp.clip(array, -limit, limit).astype(held_as)


def heavy_noise(own_key, shape, scale, bound, cuts, heavy, kind=jnp.bfloat16):
    result = scale * jax.random.normal(own_key, shape, jnp.float32)
    if cuts:
        result = result * block_levels(own_key, shape, cuts, -0.22, 0.18)
    return jnp.clip(spiked(result, jax.random.fold_in(own_key, 3), *heavy), -bound, bound).astype(kind)


def setup_inputs(seed: int = 0) -> dict:
    key_of = jax.random.split(jax.random.key(seed), 14)
    bem_tiles = heavy_noise(key_of[0], (NS, NS), (4 * NS) ** -0.5, 0.03125, ((0, 8), (1, 16)), (1, 0, 16, 2.0), jnp.float32)
    leaf_inverse = draw_leaf_inverse(jax.random.fold_in(key_of[13], 71), 0)
    coupling = gaussian(key_of[2], (GROUPS, NSUBD, LEAF, SEP), (8 * LEAF) ** -0.5, 0.0625, ((0, 8), (1, 16)), jnp.float32)
    schur_inverse = draw_schur_inverse(jax.random.fold_in(key_of[13], 71), 0)
    leaf_load = gaussian(key_of[4], (GROUPS, NSUBD, LEAF, LOADS), 1.0, 6.0, ((0, 8), (1, 16)), jnp.float32)
    sep_load = gaussian(key_of[5], (GROUPS, SEP, LOADS), 1.0, 6.0, ((0, 8),), jnp.float32)
    surf_load = gaussian(key_of[6], (NS, LOADS), 1.0, 6.0, ((0, 128),), jnp.float32)
    surf_start = gaussian(key_of[7], (NS, LOADS), 1.0, 6.0, ((0, 128),), jnp.float32)
    flux_weight = jnp.clip(jnp.exp(math.log(1.0) - 1.3862944 * jax.random.uniform(key_of[8], (GROUPS, NSUBD, MAXB, SURF_DEV), jnp.float32) ** block_levels(key_of[8], (GROUPS, NSUBD, MAXB, SURF_DEV), ((0, 8), (1, 16)), -0.2, 0.2)), 0.25, 1.0)
    trace_weight = jnp.clip(jnp.exp(math.log(1.0) - 1.3862944 * jax.random.uniform(key_of[9], (GROUPS, NSUBD, MAXB, SURF_DEV), jnp.float32) ** block_levels(key_of[9], (GROUPS, NSUBD, MAXB, SURF_DEV), ((0, 8), (1, 16)), -0.2, 0.2)), 0.25, 1.0)
    leaf_sizes = with_ends(jax.random.randint(key_of[10], (GROUPS, NSUBD), LEAF // 2, LEAF + 1), jax.random.fold_in(key_of[10], 1), LEAF // 2, LEAF).astype(jnp.int32)
    block_counts = with_ends(jax.random.randint(key_of[11], (GROUPS, NSUBD), MAXB // 2, MAXB + 1), jax.random.fold_in(key_of[11], 1), MAXB // 2, MAXB).astype(jnp.int32)
    block_owner_keys = jax.random.split(jax.random.fold_in(key_of[12], 1), GROUPS * NSUBD * MAXB // (SUB_DEV * MAXB))
    block_owner_turns = jax.random.permutation(jax.random.fold_in(key_of[12], 3), GROUPS * NSUBD * MAXB // (SUB_DEV * MAXB))
    block_owner = jax.vmap(lambda own, number: deal_out(jax.random.fold_in(key_of[12], 2), own, number, SUB_DEV * MAXB, N_SUB, 1, CAP, 2))(block_owner_keys, block_owner_turns).reshape((GROUPS, NSUBD, MAXB, 1))
    return {"bem_tiles": bem_tiles, "leaf_inverse": leaf_inverse, "coupling": coupling, "schur_inverse": schur_inverse, "leaf_load": leaf_load, "sep_load": sep_load, "surf_load": surf_load, "surf_start": surf_start, "flux_weight": flux_weight, "trace_weight": trace_weight, "leaf_sizes": leaf_sizes, "block_counts": block_counts, "block_owner": block_owner}


def reference(bem_tiles, leaf_inverse, coupling, schur_inverse, leaf_load, sep_load, surf_load, surf_start, flux_weight, trace_weight, leaf_sizes, block_counts, block_owner):
    highest = lax.Precision.HIGHEST
    mask = (jnp.arange(LEAF, dtype=jnp.int32)[None, None, :] < leaf_sizes[:, :, None]).astype(jnp.float32)
    active = (jnp.arange(MAXB, dtype=jnp.int32)[None, None, :] < block_counts[:, :, None]).astype(jnp.float32)
    picker = (block_owner[..., 0][..., None] == jnp.arange(N_SUB, dtype=jnp.int32)[None, None, None, :]).astype(jnp.float32)
    live_pick = picker * active[..., None]
    trace_scale = trace_weight * active[..., None]
    pressure = surf_start
    sep_value = jnp.zeros((GROUPS, SEP, LOADS), jnp.float32)
    solution = jnp.zeros((GROUPS, NSUBD, LEAF, LOADS), jnp.float32)
    for sweep in range(SWEEPS):
        blocks_surface = pressure.reshape(GROUPS, N_SUB, SURF_DEV, LOADS)
        tiled = jnp.transpose(blocks_surface, (1, 0, 2, 3)).reshape(NS, LOADS)
        applied = jnp.dot(bem_tiles, tiled, precision=highest, preferred_element_type=jnp.float32)
        flux = jnp.einsum("gjko,goil->gjkil", live_pick, blocks_surface, precision=highest) * flux_weight[..., None]
        flux = flux.reshape(GROUPS, NSUBD, LEAF, LOADS)
        pulled = jnp.einsum("gjrs,gsl->gjrl", coupling, sep_value, precision=highest)
        rhs = (leaf_load - pulled - flux) * mask[..., None]
        solution = jnp.einsum("gjrc,gjcl->gjrl", leaf_inverse, rhs, precision=highest) * mask[..., None]
        total = jnp.einsum("gjrs,gjrl->gsl", coupling, solution, precision=highest)
        sep_value = jnp.einsum("gst,gtl->gsl", schur_inverse, sep_load - total, precision=highest)
        weighted = solution.reshape(GROUPS, NSUBD, MAXB, SURF_DEV, LOADS) * trace_scale[..., None]
        trace = jnp.einsum("gjko,gjkil->goil", picker, weighted, precision=highest).reshape(NS, LOADS)
        pressure = surf_load + applied + trace
    return solution, sep_value, pressure
```

```python
import jax
import jax.numpy as jnp
from jax import lax
from jax.sharding import PartitionSpec as P

SWEEPS = 3
PREC = lax.Precision.HIGH


def mm(spec, a, b):
    return jnp.einsum(spec, a, b, precision=PREC, preferred_element_type=jnp.float32)


def on_device(
    bem_tiles,
    leaf_inverse,
    coupling,
    schur_inverse,
    leaf_load,
    sep_load,
    surf_load,
    surf_start,
    flux_weight,
    trace_weight,
    leaf_sizes,
    block_counts,
    block_owner,
):
    parts = lax.axis_size("sub")
    here = lax.axis_index("sub")
    core = lax.rem(here, 2)
    chips = parts // 2
    width, loads = surf_load.shape
    leaves, order = leaf_inverse.shape[1:3]
    blocks = order // width
    entries = leaves * blocks
    separator = schur_inverse.shape[1]
    share = schur_inverse.shape[2]
    same_core = [[2 * c + k for c in range(chips)] for k in range(2)]
    swap = [(i, i ^ 1) for i in range(parts)]

    def halves(z):
        pairs = z.reshape(chips, 2, *z.shape[1:])
        mine = jnp.where(core == 0, pairs[:, 0], pairs[:, 1])
        other = jnp.where(core == 0, pairs[:, 1], pairs[:, 0])
        return mine, other

    def summed(z):
        mine, other = halves(z)
        mine = mine + lax.ppermute(other, "sub", swap)
        got = lax.all_to_all(mine, "sub", 0, 0, axis_index_groups=same_core, tiled=True)
        return got.sum(0)

    def gathered(x):
        wide = jnp.broadcast_to(x[None], (chips, *x.shape))
        mine = lax.all_to_all(wide, "sub", 0, 0, axis_index_groups=same_core, tiled=True)
        other = lax.ppermute(mine, "sub", swap)
        pairs = jnp.where(
            core == 0, jnp.stack([mine, other], 1), jnp.stack([other, mine], 1)
        )
        return pairs.reshape(parts, *x.shape)

    row_mask = (jnp.arange(order, dtype=jnp.int32)[None, :] < leaf_sizes[0][:, None]).astype(
        jnp.float32
    )[:, :, None]
    active = (
        (jnp.arange(blocks, dtype=jnp.int32)[None, :] < block_counts[0][:, None])
        .astype(jnp.float32)
        .reshape(entries)
    )
    owner = block_owner[0, :, :, 0].reshape(entries)
    picker = (owner[:, None] == jnp.arange(parts, dtype=jnp.int32)[None, :]).astype(jnp.float32)
    flux_scale = (flux_weight[0].reshape(entries, width) * active[:, None])[:, :, None]
    trace_scale = (trace_weight[0].reshape(entries, width) * active[:, None])[:, :, None]

    schur_t = lax.all_gather(schur_inverse[0].T, "sub", axis=0, tiled=True)
    pressure = surf_start
    payload = surf_start
    for sweep in range(SWEEPS):
        spread = gathered(payload)
        column = lax.all_to_all(
            jnp.broadcast_to(pressure[None], (lax.axis_size("grp"), *pressure.shape)),
            "grp", 0, 0, tiled=True,
        ).reshape(-1, loads)
        surface = spread[:, :width]
        flux = mm("eo,oil->eil", picker, surface) * flux_scale
        rhs = leaf_load[0] - flux.reshape(leaves, order, loads)
        if sweep:
            total = spread[:, width:].reshape(separator, loads)
            sep_value = mm("ts,tl->sl", schur_t, sep_load[0] - total)
            rhs = rhs - mm("jrs,sl->jrl", coupling[0], sep_value)
        solution = mm("jrc,jcl->jrl", leaf_inverse[0], rhs * row_mask) * row_mask
        part = mm("jrs,jrl->sl", coupling[0], solution)
        if sweep == SWEEPS - 1:
            part = mm("ts,tl->sl", schur_t, part)
        weighted = solution.reshape(entries, width, loads) * trace_scale
        dense = mm("eo,eil->oil", picker, weighted)
        applied = mm("rc,cl->rl", bem_tiles, column).reshape(parts, width, loads)
        payload = summed(
            jnp.concatenate([applied + dense, part.reshape(parts, share, loads)], axis=1)
        )
        pressure = surf_load + payload[:width]
        payload = jnp.concatenate([pressure, payload[width:]], axis=0)
    own = mm("ts,tl->sl", lax.dynamic_slice_in_dim(schur_t, here * share, share, 1), sep_load[0])
    return (solution[None], (own - payload[width:])[None], pressure)


def solution(mesh):
    return jax.shard_map(
        on_device,
        mesh=mesh,
        in_specs=(
            P("grp", "sub"),
            P("grp", "sub", None, None),
            P("grp", "sub", None, None),
            P("grp", None, "sub"),
            P("grp", "sub", None, None),
            P("grp", None, None),
            P(("grp", "sub"), None),
            P(("grp", "sub"), None),
            P("grp", "sub", None, None),
            P("grp", "sub", None, None),
            P("grp", "sub"),
            P("grp", "sub"),
            P("grp", "sub", None, None),
        ),
        out_specs=(P("grp", "sub", None, None), P("grp", "sub", None), P(("grp", "sub"), None)),
        check_vma=False,
    )
```

```python
import functools

import jax
import jax.numpy as jnp
from jax import lax
from jax.experimental import pallas as pl
from jax.experimental.pallas import tpu as pltpu
from jax.sharding import PartitionSpec as P

SWEEPS = 3
F32, BF16 = jnp.float32, jnp.bfloat16
VM = pl.BlockSpec(memory_space=pltpu.VMEM)
SM = pl.BlockSpec(memory_space=pltpu.SMEM)
AN = pl.BlockSpec(memory_space=pltpu.HBM)
MIB = 2**20


GRP_STEPS = (4, 1, 3)
SUB_STEPS = (2, 4, 12, 1)


def origins(steps):
    found = [0]
    for step in steps:
        found += [step ^ origin for origin in found]
    return found


def call(body, name, out, ins, scratch=(), limit=6, flops=0, moved=0):
    return pl.pallas_call(
        body,
        out_shape=out,
        in_specs=ins,
        out_specs=jax.tree.map(lambda _: VM, out),
        scratch_shapes=list(scratch),
        compiler_params=pltpu.CompilerParams(vmem_limit_bytes=limit * MIB),
        cost_estimate=pl.CostEstimate(flops=flops, bytes_accessed=moved, transcendentals=0),
        name=name,
    )


def shaped(shape, dtype=F32):
    return jax.ShapeDtypeStruct(shape, dtype)


def parted(x):
    hi = x.astype(BF16)
    return hi, (x - hi.astype(F32)).astype(BF16)


def widened(x):
    return jnp.concatenate(parted(x), axis=1)


def dot(a, b):
    return jnp.dot(a, b, preferred_element_type=F32)


def product(hi, lo, wide):
    n = wide.shape[1] // 2
    both = dot(hi, wide)
    return both[:, :n] + both[:, n:] + dot(lo, wide[:, :n])


def streamed(src, buf, sems, tile, use):
    slots = buf.shape[0]
    count = src.shape[0] // tile

    def copy(i, slot):
        return pltpu.make_async_copy(src.at[pl.ds(i * tile, tile)], buf.at[slot], sems.at[slot])

    for i in range(min(slots, count)):
        copy(i, i).start()
    for i in range(count):
        copy(i, i % slots).wait()
        use(i, buf[i % slots])
        if i + slots < count:
            copy(i + slots, i % slots).start()


def split_rows(tile, src, hi_ref, lo_ref, buf, sems):
    def use(i, x):
        rows = slice(i * tile, (i + 1) * tile)
        hi_ref[rows], lo_ref[rows] = parted(x)

    streamed(src, buf, sems, tile, use)


def split_cores(tile, width, src, hi_ref, lo_ref, buf, sems):
    def use(i, x):
        for b in range(tile // width):
            block = i * (tile // width) + b
            chip, core = block // 2, block % 2
            rows = slice(chip * width, (chip + 1) * width)
            hi, lo = parted(x[b * width : (b + 1) * width])
            hi_ref[core, rows], lo_ref[core, rows] = hi, lo

    streamed(src, buf, sems, tile, use)


def split_turned(tile, src, hi_ref, lo_ref, hi_t_ref, lo_t_ref, buf, sems):
    def use(i, x):
        rows = slice(i * tile, (i + 1) * tile)
        hi_ref[rows], lo_ref[rows] = parted(x)
        hi_t_ref[:, rows], lo_t_ref[:, rows] = parted(x.T)

    streamed(src, buf, sems, tile, use)


def split_call(x, body, name, outs, tile):
    slots = 4
    return call(
        body,
        name,
        tuple(shaped(s, BF16) for s in outs),
        [AN],
        [pltpu.VMEM((slots, tile, x.shape[1]), F32), pltpu.SemaphoreType.DMA((slots,))],
        limit=8,
        moved=4 * x.size,
    )(x)


def laid(pieces, steps, here, whole):
    rows = pieces[0].shape[0]
    block = 0
    for piece in pieces:
        for i in range(piece.shape[0] // rows):
            at = pl.multiple_of((here ^ origins(steps)[block]) * rows, rows)
            whole[pl.ds(at, rows)] = piece[i * rows : (i + 1) * rows]
            block += 1


def turn_kernel(here_ref, *rest):
    *pieces, hi_ref, lo_ref, whole = rest
    laid(pieces, SUB_STEPS, here_ref[0], whole)
    hi_ref[...], lo_ref[...] = parted(whole[...].T)


def leaf_kernel(
    width, first, last,
    here_ref, owner_ref, size_ref,
    load, flux_t, trace_t, inv_hi, inv_lo, cpl_t_hi, cpl_t_lo, sep_load,
    *rest,
):
    if first:
        *rest, field = rest
    *rest, sol, dense, part, gathered, wide, wide_sol = rest
    leaves, order, loads = load.shape
    blocks = order // width
    chips = dense.shape[1]
    share = part.shape[0] // (2 * chips)
    here = here_ref[0]
    core = here % 2

    if first:
        laid(rest, SUB_STEPS, here, field)

        def surface(o):
            return field[pl.ds(pl.multiple_of(o * width, width), width)]

    else:
        cpl_hi, cpl_lo, sch_hi, sch_lo, mine, other = rest

        def surface(o):
            chip = o // 2
            return jnp.where(o - 2 * chip == core, mine[chip, :width], other[chip, :width])

    if not first:
        for chip in range(chips):
            a, b = mine[chip, width:], other[chip, width:]
            at = 2 * chip * share
            gathered[at : at + share] = jnp.where(core == 0, a, b)
            gathered[at + share : at + 2 * share] = jnp.where(core == 0, b, a)
        sep_wide = widened(product(sch_hi[...], sch_lo[...], widened(gathered[...])))
    dense[...] = jnp.zeros_like(dense)
    for j in range(leaves):
        rows = slice(j * order, (j + 1) * order)
        if not first:
            pulled = product(cpl_hi[rows], cpl_lo[rows], sep_wide)
        for k in range(blocks):
            e = j * blocks + k
            o = owner_ref[e]
            at = slice(k * width, (k + 1) * width)
            rhs = load[j, at] - surface(o) * flux_t[:, e : e + 1]
            if not first:
                rhs = rhs - pulled[at]
            row = k * width + lax.broadcasted_iota(jnp.int32, (width, loads), 0)
            wide[at] = widened(jnp.where(row < size_ref[j], rhs, 0.0))
        got = product(inv_hi[rows], inv_lo[rows], wide[...])
        for k in range(blocks):
            e = j * blocks + k
            o = owner_ref[e]
            chip = o // 2
            at = slice(k * width, (k + 1) * width)
            row = k * width + lax.broadcasted_iota(jnp.int32, (width, loads), 0)
            block = jnp.where(row < size_ref[j], got[at], 0.0)
            sol[j, at] = block
            dense[o - 2 * chip, chip] += block * trace_t[:, e : e + 1]
            wide_sol[j * order + k * width : j * order + (k + 1) * width] = widened(block)
    left = jnp.where(here == 0, sep_load[...], 0.0) - product(
        cpl_t_hi[...], cpl_t_lo[...], wide_sol[...]
    )
    if last:
        left = product(sch_hi[...], sch_lo[...], widened(left))
    part[...] = left


def surface_kernel(width, pick_ref, group_ref, hi, lo, *rest):
    *pieces, dense, part, out, wide = rest
    pick = pick_ref[0]
    chips = out.shape[0]
    share = part.shape[0] // (2 * chips)
    block = 0
    for piece in pieces:
        for i in range(piece.shape[0] // width):
            at = pl.multiple_of((group_ref[0] ^ origins(GRP_STEPS)[block]) * width, width)
            wide[pl.ds(at, width)] = widened(piece[i * width : (i + 1) * width])
            block += 1
    got = product(hi[pick], lo[pick], wide[...])
    for chip in range(chips):
        out[chip, :width] = dense[pick, chip] + got[chip * width : (chip + 1) * width]
        at = pl.multiple_of((2 * chip + pick) * share, share)
        out[chip, width:] = part[pl.ds(at, share)]


def total_kernel(width, got, load, wide, again):
    chips = got.shape[0]
    total = got[0]
    for chip in range(1, chips):
        total = total + got[chip]
    field = load[...] + total[:width]
    for chip in range(chips):
        wide[chip, :width] = field
        wide[chip, width:] = total[width:]
    again[...] = field


def final_kernel(width, got, load, field, separator):
    total = got[0]
    for chip in range(1, got.shape[0]):
        total = total + got[chip]
    field[...] = load[...] + total[:width]
    separator[...] = total[width:]


def on_device(
    bem_tiles,
    leaf_inverse,
    coupling,
    schur_inverse,
    leaf_load,
    sep_load,
    surf_load,
    surf_start,
    flux_weight,
    trace_weight,
    leaf_sizes,
    block_counts,
    block_owner,
):
    parts = lax.axis_size("sub")
    here = lax.axis_index("sub")
    core = lax.rem(here, 2).astype(jnp.int32)
    mine_id, other_id = core.reshape(1), (1 - core).reshape(1)
    here_id = here.astype(jnp.int32).reshape(1)
    group = lax.axis_index("grp").astype(jnp.int32).reshape(1)
    chips = parts // 2
    width, loads = surf_load.shape
    leaves, order = leaf_inverse.shape[1:3]
    blocks = order // width
    entries = leaves * blocks
    separator = schur_inverse.shape[1]
    share = schur_inverse.shape[2]
    rows = bem_tiles.shape[0]
    columns = bem_tiles.shape[1]
    same_core = [[2 * c + k for c in range(chips)] for k in range(2)]
    swap = [(i, i ^ 1) for i in range(parts)]

    def over_chips(x):
        return lax.all_to_all(x, "sub", 0, 0, axis_index_groups=same_core, tiled=True)

    def doubled(x, axis, steps):
        size = lax.axis_size(axis)
        pieces = [x]
        for step in steps:
            held = pieces[0] if len(pieces) == 1 else jnp.concatenate(pieces, axis=0)
            pieces.append(lax.ppermute(held, axis, [(i, i ^ step) for i in range(size)]))
        return pieces

    inv = leaf_inverse.reshape(leaves * order, order)
    cpl = coupling.reshape(leaves * order, separator)
    inv_hi, inv_lo = split_call(
        inv, functools.partial(split_rows, 256), "split_leaf", [inv.shape] * 2, 256
    )
    cpl_hi, cpl_lo, cpl_t_hi, cpl_t_lo = split_call(
        cpl, functools.partial(split_turned, 256), "split_coupling",
        [cpl.shape] * 2 + [cpl.shape[::-1]] * 2, 256,
    )
    bem_hi, bem_lo = split_call(
        bem_tiles, functools.partial(split_cores, 2 * width, width), "split_surface",
        [(2, rows // 2, columns)] * 2, 2 * width,
    )
    active = (
        (jnp.arange(blocks, dtype=jnp.int32)[None, :] < block_counts[0][:, None])
        .astype(F32)
        .reshape(entries, 1)
    )
    owner = block_owner.reshape(entries)
    sizes = leaf_sizes.reshape(leaves)
    flux_t = (flux_weight.reshape(entries, width) * active).T
    trace_t = (trace_weight.reshape(entries, width) * active).T
    field = surf_start
    for sweep in range(SWEEPS):
        first, last = sweep == 0, sweep == SWEEPS - 1
        if first:
            known = doubled(surf_start, "sub", SUB_STEPS)
        else:
            mine = over_chips(wide)
            mine, field = lax.optimization_barrier((mine, field))
            known = [mine, lax.ppermute(mine, "sub", swap)]
        pieces = doubled(field, "grp", GRP_STEPS)
        if first:
            schur_pieces = doubled(schur_inverse[0].T, "sub", SUB_STEPS)
            sch_hi, sch_lo = call(
                turn_kernel, "split_schur", (shaped((separator, separator), BF16),) * 2,
                [SM] + [VM] * len(schur_pieces),
                [pltpu.VMEM((separator, separator), F32)],
                moved=8 * separator * separator,
            )(here_id, *schur_pieces)
        operands = [here_id, owner, sizes, leaf_load[0], flux_t, trace_t]
        operands += [inv_hi, inv_lo, cpl_t_hi, cpl_t_lo, sep_load[0]]
        if not first:
            operands += [cpl_hi, cpl_lo, sch_hi, sch_lo]
        operands += known
        solution, dense, part = call(
            functools.partial(leaf_kernel, width, first, last),
            "leaves",
            (
                shaped((leaves, order, loads)),
                shaped((2, chips, width, loads)),
                shaped((separator, loads)),
            ),
            [SM] * 3 + [VM] * (len(operands) - 3),
            [
                pltpu.VMEM((separator, loads), F32),
                pltpu.VMEM((order, 2 * loads), BF16),
                pltpu.VMEM((leaves * order, 2 * loads), BF16),
            ]
            + ([pltpu.VMEM((parts * width, loads), F32)] if first else []),
            limit=12,
            flops=8 * leaves * order * loads * (order + 2 * separator),
            moved=16 * MIB,
        )(*operands)

        def surface(pick):
            return call(
                functools.partial(surface_kernel, width),
                "surface",
                shaped((chips, width + share, loads)),
                [SM] * 2 + [VM] * (4 + len(pieces)),
                [pltpu.VMEM((columns, 2 * loads), BF16)],
                limit=8,
                flops=4 * rows * columns * loads,
                moved=6 * MIB,
            )(pick, group, bem_hi, bem_lo, *pieces, dense, part)

        swapped = lax.ppermute(surface(other_id), "sub", swap)
        payload = surface(mine_id) + swapped
        if first:
            payload, sch_hi, sch_lo = lax.optimization_barrier((payload, sch_hi, sch_lo))
        got = over_chips(payload)
        if not last:
            wide, field = call(
                functools.partial(total_kernel, width),
                "total",
                (shaped((chips, width + share, loads)), shaped((width, loads))),
                [VM] * 2,
                moved=2 * MIB,
            )(got, surf_load)
    pressure, sep_rows = call(
        functools.partial(final_kernel, width),
        "final",
        (shaped((width, loads)), shaped((share, loads))),
        [VM] * 2,
        moved=MIB,
    )(got, surf_load)
    return (solution[None], sep_rows[None], pressure)


def solution(mesh):
    return jax.shard_map(
        on_device,
        mesh=mesh,
        in_specs=(
            P("grp", "sub"),
            P("grp", "sub", None, None),
            P("grp", "sub", None, None),
            P("grp", None, "sub"),
            P("grp", "sub", None, None),
            P("grp", None, None),
            P(("grp", "sub"), None),
            P(("grp", "sub"), None),
            P("grp", "sub", None, None),
            P("grp", "sub", None, None),
            P("grp", "sub"),
            P("grp", "sub"),
            P("grp", "sub", None, None),
        ),
        out_specs=(P("grp", "sub", None, None), P("grp", "sub", None), P(("grp", "sub"), None)),
        check_vma=False,
    )
```

```python
import functools

import jax
import jax.numpy as jnp
from jax import lax
from jax.experimental import pallas as pl
from jax.experimental.pallas import tpu as pltpu
from jax.sharding import PartitionSpec as P

SWEEPS = 3
F32, BF16 = jnp.float32, jnp.bfloat16
VM = pl.BlockSpec(memory_space=pltpu.VMEM)
SM = pl.BlockSpec(memory_space=pltpu.SMEM)
AN = pl.BlockSpec(memory_space=pltpu.HBM)
MIB = 2**20


GRP_STEPS = (4, 1, 3)


def origins(steps):
    found = [0]
    for step in steps:
        found += [step ^ origin for origin in found]
    return found


def call(body, name, out, ins, scratch=(), limit=6, flops=0, moved=0):
    return pl.pallas_call(
        body,
        out_shape=out,
        in_specs=ins,
        out_specs=jax.tree.map(lambda _: VM, out),
        scratch_shapes=list(scratch),
        compiler_params=pltpu.CompilerParams(vmem_limit_bytes=limit * MIB),
        cost_estimate=pl.CostEstimate(flops=flops, bytes_accessed=moved, transcendentals=0),
        name=name,
    )


def shaped(shape, dtype=F32):
    return jax.ShapeDtypeStruct(shape, dtype)


def parted(x):
    hi = x.astype(BF16)
    return hi, (x - hi.astype(F32)).astype(BF16)


def widened(x):
    return jnp.concatenate(parted(x), axis=1)


def dot(a, b):
    return jnp.dot(a, b, preferred_element_type=F32)


def product(hi, lo, wide):
    n = wide.shape[1] // 2
    both = dot(hi, wide)
    return both[:, :n] + both[:, n:] + dot(lo, wide[:, :n])


def streamed(src, buf, sems, tile, use):
    slots = buf.shape[0]
    count = src.shape[0] // tile

    def copy(i, slot):
        return pltpu.make_async_copy(src.at[pl.ds(i * tile, tile)], buf.at[slot], sems.at[slot])

    for i in range(min(slots, count)):
        copy(i, i).start()
    for i in range(count):
        copy(i, i % slots).wait()
        use(i, buf[i % slots])
        if i + slots < count:
            copy(i + slots, i % slots).start()


def split_rows(tile, token, src, hi_ref, lo_ref, buf, sems):
    def use(i, x):
        rows = slice(i * tile, (i + 1) * tile)
        hi_ref[rows], lo_ref[rows] = parted(x)

    streamed(src, buf, sems, tile, use)


def split_cores(tile, width, token, src, hi_ref, lo_ref, buf, sems):
    def use(i, x):
        for b in range(tile // width):
            block = i * (tile // width) + b
            chip, core = block // 2, block % 2
            rows = slice(chip * width, (chip + 1) * width)
            hi, lo = parted(x[b * width : (b + 1) * width])
            hi_ref[core, rows], lo_ref[core, rows] = hi, lo

    streamed(src, buf, sems, tile, use)


def split_turned(tile, token, src, hi_ref, lo_ref, hi_t_ref, lo_t_ref, buf, sems):
    def use(i, x):
        rows = slice(i * tile, (i + 1) * tile)
        hi_ref[rows], lo_ref[rows] = parted(x)
        hi_t_ref[:, rows], lo_t_ref[:, rows] = parted(x.T)

    streamed(src, buf, sems, tile, use)


def split_call(token, x, body, name, outs, tile):
    slots = 4
    return call(
        body,
        name,
        tuple(shaped(s, BF16) for s in outs),
        [SM, AN],
        [pltpu.VMEM((slots, tile, x.shape[1]), F32), pltpu.SemaphoreType.DMA((slots,))],
        limit=8,
        moved=4 * x.size,
    )(token, x)


def start_kernel(width, field, schur_t, wide):
    share, columns = schur_t.shape
    for chip in range(wide.shape[0]):
        wide[chip, :width] = field[...]
        for q in range(columns // width):
            rows = slice(width + q * share, width + (q + 1) * share)
            wide[chip, rows] = schur_t[:, q * width : (q + 1) * width]


def turn_kernel(width, core_ref, mine, other, hi_ref, lo_ref, whole):
    chips = mine.shape[0]
    columns = whole.shape[1]
    share = whole.shape[0] // (2 * chips)
    core = core_ref[0]
    for chip in range(chips):
        at = 2 * chip * share
        for q in range(columns // width):
            rows = slice(width + q * share, width + (q + 1) * share)
            to = slice(q * width, (q + 1) * width)
            a, b = mine[chip, rows], other[chip, rows]
            whole[at : at + share, to] = jnp.where(core == 0, a, b)
            whole[at + share : at + 2 * share, to] = jnp.where(core == 0, b, a)
    hi_ref[...], lo_ref[...] = parted(whole[...].T)


def leaf_kernel(
    width, first, last,
    here_ref, owner_ref, size_ref, count_ref,
    load, flux_weight, trace_weight, inv_hi, inv_lo, cpl_t_hi, cpl_t_lo, sep_load, mine, other,
    *rest,
):
    if not first:
        cpl_hi, cpl_lo, sch_hi, sch_lo, *rest = rest
    sol, dense, part, gathered, wide, wide_sol = rest
    leaves, order, loads = load.shape
    blocks = order // width
    chips = dense.shape[1]
    share = part.shape[0] // (2 * chips)
    here = here_ref[0]
    core = here % 2
    flux_t, trace_t = flux_weight[...].T, trace_weight[...].T

    def scale(turned, j, k):
        e = j * blocks + k
        return jnp.where(k < count_ref[0, j], turned[:, e : e + 1], 0.0)

    def surface(o):
        chip = o // 2
        return jnp.where(o - 2 * chip == core, mine[chip, :width], other[chip, :width])

    if not first:
        for chip in range(chips):
            a, b = mine[chip, width:], other[chip, width:]
            at = 2 * chip * share
            gathered[at : at + share] = jnp.where(core == 0, a, b)
            gathered[at + share : at + 2 * share] = jnp.where(core == 0, b, a)
        sep_wide = widened(product(sch_hi[...], sch_lo[...], widened(gathered[...])))
    dense[...] = jnp.zeros_like(dense)
    for j in range(leaves):
        rows = slice(j * order, (j + 1) * order)
        if not first:
            pulled = product(cpl_hi[rows], cpl_lo[rows], sep_wide)
        for k in range(blocks):
            o = owner_ref[j * blocks + k]
            at = slice(k * width, (k + 1) * width)
            rhs = load[j, at] - surface(o) * scale(flux_t, j, k)
            if not first:
                rhs = rhs - pulled[at]
            row = k * width + lax.broadcasted_iota(jnp.int32, (width, loads), 0)
            wide[at] = widened(jnp.where(row < size_ref[0, j], rhs, 0.0))
        got = product(inv_hi[rows], inv_lo[rows], wide[...])
        for k in range(blocks):
            o = owner_ref[j * blocks + k]
            chip = o // 2
            at = slice(k * width, (k + 1) * width)
            row = k * width + lax.broadcasted_iota(jnp.int32, (width, loads), 0)
            block = jnp.where(row < size_ref[0, j], got[at], 0.0)
            sol[j, at] = block
            dense[o - 2 * chip, chip] += block * scale(trace_t, j, k)
            wide_sol[j * order + k * width : j * order + (k + 1) * width] = widened(block)
    left = jnp.where(here == 0, sep_load[...], 0.0) - product(
        cpl_t_hi[...], cpl_t_lo[...], wide_sol[...]
    )
    if last:
        left = product(sch_hi[...], sch_lo[...], widened(left))
    part[...] = left


def surface_kernel(width, pick_ref, group_ref, hi, lo, *rest):
    *pieces, dense, part, out, wide = rest
    pick = pick_ref[0]
    chips = out.shape[0]
    share = part.shape[0] // (2 * chips)
    block = 0
    for piece in pieces:
        for i in range(piece.shape[0] // width):
            at = pl.multiple_of((group_ref[0] ^ origins(GRP_STEPS)[block]) * width, width)
            wide[pl.ds(at, width)] = widened(piece[i * width : (i + 1) * width])
            block += 1
    got = product(hi[pick], lo[pick], wide[...])
    for chip in range(chips):
        out[chip, :width] = dense[pick, chip] + got[chip * width : (chip + 1) * width]
        at = pl.multiple_of((2 * chip + pick) * share, share)
        out[chip, width:] = part[pl.ds(at, share)]


def summed(got, rows):
    total = got[0, rows]
    for chip in range(1, got.shape[0]):
        total = total + got[chip, rows]
    return total


def field_kernel(width, got, load, field):
    field[...] = load[...] + summed(got, slice(0, width))


def wide_kernel(width, got, field, wide):
    rest = summed(got, slice(width, None))
    for chip in range(wide.shape[0]):
        wide[chip, :width] = field[...]
        wide[chip, width:] = rest


def final_kernel(width, got, load, field, separator):
    field[...] = load[...] + summed(got, slice(0, width))
    separator[...] = summed(got, slice(width, None))


def on_device(
    bem_tiles,
    leaf_inverse,
    coupling,
    schur_inverse,
    leaf_load,
    sep_load,
    surf_load,
    surf_start,
    flux_weight,
    trace_weight,
    leaf_sizes,
    block_counts,
    block_owner,
):
    parts = lax.axis_size("sub")
    groups = lax.axis_size("grp")
    here = lax.axis_index("sub")
    core = lax.rem(here, 2).astype(jnp.int32)
    mine_id, other_id = core.reshape(1), (1 - core).reshape(1)
    here_id = here.astype(jnp.int32).reshape(1)
    group = lax.axis_index("grp").astype(jnp.int32).reshape(1)
    chips = parts // 2
    width, loads = surf_load.shape
    leaves, order = leaf_inverse.shape[1:3]
    blocks = order // width
    entries = leaves * blocks
    separator = schur_inverse.shape[1]
    share = schur_inverse.shape[2]
    rows = bem_tiles.shape[0]
    columns = bem_tiles.shape[1]
    same_core = [[2 * c + k for c in range(chips)] for k in range(2)]
    swap = [(i, i ^ 1) for i in range(parts)]

    def over_chips(x):
        return lax.all_to_all(x, "sub", 0, 0, axis_index_groups=same_core, tiled=True)

    def more(pieces, step):
        held = jnp.concatenate(pieces, axis=0) if len(pieces) > 1 else pieces[0]
        return [*pieces, lax.ppermute(held, "grp", [(i, i ^ step) for i in range(groups)])]

    inv = leaf_inverse.reshape(leaves * order, order)
    cpl = coupling.reshape(leaves * order, separator)
    field = surf_start
    wide = call(
        functools.partial(start_kernel, width),
        "start",
        shaped((chips, 2 * width, loads)),
        [VM] * 2,
        moved=MIB,
    )(surf_start, schur_inverse[0].T)
    wide, here_id, mine_id, other_id, group, owner = lax.optimization_barrier(
        (wide, here_id, mine_id, other_id, group, block_owner.reshape(entries))
    )
    for sweep in range(SWEEPS):
        first, last = sweep == 0, sweep == SWEEPS - 1
        pieces = [field]
        if first:
            mine = over_chips(wide)
        else:
            pieces = more(pieces, GRP_STEPS[0])
            wide, *pieces = lax.optimization_barrier((wide, *pieces))
            mine = over_chips(wide)
        mine, token, *pieces = lax.optimization_barrier((mine, here_id, *pieces))
        for step in GRP_STEPS[len(pieces) - 1 :]:
            pieces = more(pieces, step)
        other = lax.ppermute(mine, "sub", swap)
        if first:
            inv_hi, inv_lo = split_call(
                token, inv, functools.partial(split_rows, 256), "split_leaf", [inv.shape] * 2, 256
            )
            cpl_hi, cpl_lo, cpl_t_hi, cpl_t_lo = split_call(
                token, cpl, functools.partial(split_turned, 256), "split_coupling",
                [cpl.shape] * 2 + [cpl.shape[::-1]] * 2, 256,
            )
            bem_hi, bem_lo = split_call(
                token, bem_tiles, functools.partial(split_cores, 2 * width, width),
                "split_surface", [(2, rows // 2, columns)] * 2, 2 * width,
            )
            sch_hi, sch_lo = call(
                functools.partial(turn_kernel, width),
                "split_schur",
                (shaped((separator, separator), BF16),) * 2,
                [SM] + [VM] * 2,
                [pltpu.VMEM((separator, separator), F32)],
                moved=8 * separator * separator,
            )(mine_id, mine, other)
        operands = [here_id, owner, leaf_sizes, block_counts, leaf_load[0]]
        operands += [w.reshape(entries, width) for w in (flux_weight, trace_weight)]
        operands += [inv_hi, inv_lo, cpl_t_hi, cpl_t_lo, sep_load[0], mine, other]
        if not first:
            operands += [cpl_hi, cpl_lo, sch_hi, sch_lo]
        solution, dense, part = call(
            functools.partial(leaf_kernel, width, first, last),
            "leaves",
            (
                shaped((leaves, order, loads)),
                shaped((2, chips, width, loads)),
                shaped((separator, loads)),
            ),
            [SM] * 4 + [VM] * (len(operands) - 4),
            [
                pltpu.VMEM((separator, loads), F32),
                pltpu.VMEM((order, 2 * loads), BF16),
                pltpu.VMEM((leaves * order, 2 * loads), BF16),
            ],
            limit=12,
            flops=8 * leaves * order * loads * (order + 2 * separator),
            moved=16 * MIB,
        )(*operands)

        def surface(pick):
            return call(
                functools.partial(surface_kernel, width),
                "surface",
                shaped((chips, width + share, loads)),
                [SM] * 2 + [VM] * (4 + len(pieces)),
                [pltpu.VMEM((columns, 2 * loads), BF16)],
                limit=8,
                flops=4 * rows * columns * loads,
                moved=6 * MIB,
            )(pick, group, bem_hi, bem_lo, *pieces, dense, part)

        swapped = lax.ppermute(surface(other_id), "sub", swap)
        payload = surface(mine_id) + swapped
        if first:
            payload, sch_hi, sch_lo = lax.optimization_barrier((payload, sch_hi, sch_lo))
        got = over_chips(payload)
        if not last:
            field = call(
                functools.partial(field_kernel, width), "field", shaped((width, loads)), [VM] * 2,
                moved=MIB,
            )(got, surf_load)
            wide = call(
                functools.partial(wide_kernel, width),
                "wide",
                shaped((chips, width + share, loads)),
                [VM] * 2,
                moved=2 * MIB,
            )(got, field)
    pressure, sep_rows = call(
        functools.partial(final_kernel, width),
        "final",
        (shaped((width, loads)), shaped((share, loads))),
        [VM] * 2,
        moved=MIB,
    )(got, surf_load)
    return (solution[None], sep_rows[None], pressure)


def solution(mesh):
    return jax.shard_map(
        on_device,
        mesh=mesh,
        in_specs=(
            P("grp", "sub"),
            P("grp", "sub", None, None),
            P("grp", "sub", None, None),
            P("grp", None, "sub"),
            P("grp", "sub", None, None),
            P("grp", None, None),
            P(("grp", "sub"), None),
            P(("grp", "sub"), None),
            P("grp", "sub", None, None),
            P("grp", "sub", None, None),
            P("grp", "sub"),
            P("grp", "sub"),
            P("grp", "sub", None, None),
        ),
        out_specs=(P("grp", "sub", None, None), P("grp", "sub", None), P(("grp", "sub"), None)),
        check_vma=False,
    )
```

```python
import functools

import jax
import jax.numpy as jnp
from jax import lax
from jax.experimental import pallas as pl
from jax.experimental.pallas import tpu as pltpu
from jax.sharding import PartitionSpec as P

SWEEPS = 3
F32, BF16 = jnp.float32, jnp.bfloat16
VM = pl.BlockSpec(memory_space=pltpu.VMEM)
SM = pl.BlockSpec(memory_space=pltpu.SMEM)
HB = pl.BlockSpec(memory_space=pltpu.HBM)
MIB = 2**20


FIRST_STEP = 4
NEXT_STEPS = (1, 3, 2)


def origins():
    return [origin for step in (0, *NEXT_STEPS) for origin in (step, step ^ FIRST_STEP)]


def call(body, name, out, ins, scratch=(), limit=6, flops=0, moved=0):
    return pl.pallas_call(
        body,
        out_shape=out,
        in_specs=ins,
        out_specs=jax.tree.map(lambda _: VM, out),
        scratch_shapes=list(scratch),
        compiler_params=pltpu.CompilerParams(vmem_limit_bytes=limit * MIB),
        cost_estimate=pl.CostEstimate(flops=flops, bytes_accessed=moved, transcendentals=0),
        name=name,
    )


def shaped(shape, dtype=F32):
    return jax.ShapeDtypeStruct(shape, dtype)


def parted(x):
    hi = x.astype(BF16)
    return hi, (x - hi.astype(F32)).astype(BF16)


def widened(x):
    return jnp.concatenate(parted(x), axis=1)


def dot(a, b):
    return jnp.dot(a, b, preferred_element_type=F32)


def product(hi, lo, wide):
    n = wide.shape[1] // 2
    both = dot(hi, wide)
    return both[:, :n] + both[:, n:] + dot(lo, wide[:, :n])


def start_kernel(width, field, schur_t, wide):
    share, columns = schur_t.shape
    for chip in range(wide.shape[0]):
        wide[chip, :width] = field[...]
        for q in range(columns // width):
            rows = slice(width + q * share, width + (q + 1) * share)
            wide[chip, rows] = schur_t[:, q * width : (q + 1) * width]


def turn_kernel(width, core_ref, mine, other, hi_ref, lo_ref, whole):
    chips = mine.shape[0]
    columns = whole.shape[1]
    share = whole.shape[0] // (2 * chips)
    core = core_ref[0]
    for chip in range(chips):
        at = 2 * chip * share
        for q in range(columns // width):
            rows = slice(width + q * share, width + (q + 1) * share)
            to = slice(q * width, (q + 1) * width)
            a, b = mine[chip, rows], other[chip, rows]
            whole[at : at + share, to] = jnp.where(core == 0, a, b)
            whole[at + share : at + 2 * share, to] = jnp.where(core == 0, b, a)
    hi_ref[...], lo_ref[...] = parted(whole[...].T)


def leaf_kernel(
    width, first, last,
    here_ref, owner_ref, size_ref, count_ref,
    load, flux_weight, trace_weight, sep_load, mine, other, *rest,
):
    if first:
        inv, cpl, sol, dense, part, *rest = rest
        inv_hi, inv_lo, cpl_hi, cpl_lo, cpl_t_hi, cpl_t_lo, *rest = rest
        wide, wide_sol, inv_buf, cpl_buf, inv_sems, cpl_sems = rest
    else:
        inv_hi, inv_lo, cpl_t_hi, cpl_t_lo, cpl_hi, cpl_lo, sch_hi, sch_lo, *rest = rest
        sol, dense, part, wide, wide_sol, gathered = rest
    leaves, order, loads = load.shape
    blocks = order // width
    chips = dense.shape[1]
    share = part.shape[0] // (2 * chips)
    here = here_ref[0]
    core = here % 2
    flux_t, trace_t = flux_weight[...].T, trace_weight[...].T
    tile = order // 2 if first else order

    def tiles(src, buf, sems):
        return [
            pltpu.make_async_copy(src.at[pl.ds(i * tile, tile)], buf.at[i], sems.at[i])
            for i in range(src.shape[0] // tile)
        ]

    if first:
        inv_copies, cpl_copies = tiles(inv, inv_buf, inv_sems), tiles(cpl, cpl_buf, cpl_sems)
        for copy in inv_copies + cpl_copies:
            copy.start()

    def scale(turned, j, k):
        e = j * blocks + k
        return jnp.where(k < count_ref[0, j], turned[:, e : e + 1], 0.0)

    def live(j, k, x):
        row = k * width + lax.broadcasted_iota(jnp.int32, (width, loads), 0)
        return jnp.where(row < size_ref[0, j], x, 0.0)

    def surface(o):
        chip = o // 2
        return jnp.where(o - 2 * chip == core, mine[chip, :width], other[chip, :width])

    if not first:
        for chip in range(chips):
            a, b = mine[chip, width:], other[chip, width:]
            at = 2 * chip * share
            gathered[at : at + share] = jnp.where(core == 0, a, b)
            gathered[at + share : at + 2 * share] = jnp.where(core == 0, b, a)
        sep_wide = widened(product(sch_hi[...], sch_lo[...], widened(gathered[...])))
    dense[...] = jnp.zeros_like(dense)
    for j in range(leaves):
        if not first:
            rows = slice(j * order, (j + 1) * order)
            pulled = product(cpl_hi[rows], cpl_lo[rows], sep_wide)
        for k in range(blocks):
            at = slice(k * width, (k + 1) * width)
            rhs = load[j, at] - surface(owner_ref[0, j, 0, k]) * scale(flux_t, j, k)
            if not first:
                rhs = rhs - pulled[at]
            wide[j, at] = widened(live(j, k, rhs))
        for t in range(order // tile):
            start = j * order + t * tile
            rows = slice(start, start + tile)
            if first:
                i = start // tile
                inv_copies[i].wait()
                hi, lo = parted(inv_buf[i])
                inv_hi[rows], inv_lo[rows] = hi, lo
                got = product(hi, lo, wide[j])
            else:
                got = product(inv_hi[rows], inv_lo[rows], wide[j])
            for b in range(tile // width):
                k = t * (tile // width) + b
                o = owner_ref[0, j, 0, k]
                chip = o // 2
                block = live(j, k, got[b * width : (b + 1) * width])
                sol[j, k * width : (k + 1) * width] = block
                dense[o - 2 * chip, chip] += block * scale(trace_t, j, k)
                at = slice(start + b * width, start + (b + 1) * width)
                wide_sol[at] = widened(block)
    left = jnp.where(here == 0, sep_load[...], 0.0)
    if first:
        for i, copy in enumerate(cpl_copies):
            copy.wait()
            rows = slice(i * tile, (i + 1) * tile)
            cpl_hi[rows], cpl_lo[rows] = parted(cpl_buf[i])
            hi, lo = parted(cpl_buf[i].T)
            cpl_t_hi[:, rows], cpl_t_lo[:, rows] = hi, lo
            left = left - product(hi, lo, wide_sol[rows])
    else:
        left = left - product(cpl_t_hi[...], cpl_t_lo[...], wide_sol[...])
    if last:
        left = product(sch_hi[...], sch_lo[...], widened(left))
    part[...] = left


def surface_kernel(width, first, pick_ref, group_ref, *rest):
    if first:
        src, *rest, out, hi_ref, lo_ref, wide, buf, sems = rest
    else:
        hi_ref, lo_ref, *rest, out, wide = rest
    *pieces, dense, part = rest
    pick = pick_ref[0]
    chips = out.shape[0]
    share = part.shape[0] // (2 * chips)
    parts = buf.shape[0] if first else 1
    tile = chips * width // parts

    def copies(i):
        found = []
        for b in range(tile // width):
            at = pl.multiple_of((2 * (i * (tile // width) + b) + pick) * width, width)
            found.append(
                pltpu.make_async_copy(
                    src.at[pl.ds(at, width)], buf.at[i, pl.ds(b * width, width)], sems.at[i, b]
                )
            )
        return found

    if first:
        flying = [copies(i) for i in range(parts)]
        for group in flying:
            for copy in group:
                copy.start()
    block = 0
    for piece in pieces:
        for i in range(piece.shape[0] // width):
            at = pl.multiple_of((group_ref[0] ^ origins()[block]) * width, width)
            wide[pl.ds(at, width)] = widened(piece[i * width : (i + 1) * width])
            block += 1
    for i in range(parts):
        rows = slice(i * tile, (i + 1) * tile)
        if first:
            for copy in flying[i]:
                copy.wait()
            hi, lo = parted(buf[i])
            hi_ref[rows], lo_ref[rows] = hi, lo
            got = product(hi, lo, wide[...])
        else:
            got = product(hi_ref[rows], lo_ref[rows], wide[...])
        for b in range(tile // width):
            chip = i * (tile // width) + b
            out[chip, :width] = dense[pick, chip] + got[b * width : (b + 1) * width]
            at = pl.multiple_of((2 * chip + pick) * share, share)
            out[chip, width:] = part[pl.ds(at, share)]


def summed(got, rows):
    total = got[0, rows]
    for chip in range(1, got.shape[0]):
        total = total + got[chip, rows]
    return total


def field_kernel(width, got, load, field):
    field[...] = load[...] + summed(got, slice(0, width))


def wide_kernel(width, got, field, wide):
    rest = summed(got, slice(width, None))
    for chip in range(wide.shape[0]):
        wide[chip, :width] = field[...]
        wide[chip, width:] = rest


def final_kernel(width, got, load, field, separator):
    field[...] = load[...] + summed(got, slice(0, width))
    separator[...] = summed(got, slice(width, None))


def on_device(
    bem_tiles,
    leaf_inverse,
    coupling,
    schur_inverse,
    leaf_load,
    sep_load,
    surf_load,
    surf_start,
    flux_weight,
    trace_weight,
    leaf_sizes,
    block_counts,
    block_owner,
):
    parts = lax.axis_size("sub")
    groups = lax.axis_size("grp")
    here = lax.axis_index("sub")
    core = lax.rem(here, 2).astype(jnp.int32)
    mine_id, other_id = core.reshape(1), (1 - core).reshape(1)
    here_id = here.astype(jnp.int32).reshape(1)
    group = lax.axis_index("grp").astype(jnp.int32).reshape(1)
    chips = parts // 2
    width, loads = surf_load.shape
    leaves, order = leaf_inverse.shape[1:3]
    blocks = order // width
    entries = leaves * blocks
    separator = schur_inverse.shape[1]
    share = schur_inverse.shape[2]
    rows = bem_tiles.shape[0]
    columns = bem_tiles.shape[1]
    same_core = [[2 * c + k for c in range(chips)] for k in range(2)]
    swap = [(i, i ^ 1) for i in range(parts)]

    def over_chips(x):
        return lax.all_to_all(x, "sub", 0, 0, axis_index_groups=same_core, tiled=True)

    def exchanged(x, step):
        return lax.ppermute(x, "grp", [(i, i ^ step) for i in range(groups)])

    inv = leaf_inverse.reshape(leaves * order, order)
    cpl = coupling.reshape(leaves * order, separator)
    field = surf_start
    wide = call(
        functools.partial(start_kernel, width),
        "start",
        shaped((chips, 2 * width, loads)),
        [VM] * 2,
        moved=MIB,
    )(surf_start, schur_inverse[0].T)
    wide, here_id, mine_id, other_id, group, owner = lax.optimization_barrier(
        (wide, here_id, mine_id, other_id, group, block_owner.transpose(0, 1, 3, 2))
    )
    for sweep in range(SWEEPS):
        first, last = sweep == 0, sweep == SWEEPS - 1
        beyond = exchanged(field, FIRST_STEP)
        wide, beyond = lax.optimization_barrier((wide, beyond))
        mine = over_chips(wide)
        mine, field, beyond = lax.optimization_barrier((mine, field, beyond))
        pair = jnp.concatenate([field, beyond], axis=0)
        pieces = [pair] + [exchanged(pair, step) for step in NEXT_STEPS]
        other = lax.ppermute(mine, "sub", swap)
        operands = [here_id, owner, leaf_sizes, block_counts, leaf_load[0]]
        operands += [w.reshape(entries, width) for w in (flux_weight, trace_weight)]
        operands += [sep_load[0], mine, other]
        outs = [
            shaped((leaves, order, loads)),
            shaped((2, chips, width, loads)),
            shaped((separator, loads)),
        ]
        scratch = [
            pltpu.VMEM((leaves, order, 2 * loads), BF16),
            pltpu.VMEM((leaves * order, 2 * loads), BF16),
        ]
        if first:
            sch_hi, sch_lo = call(
                functools.partial(turn_kernel, width),
                "split_schur",
                (shaped((separator, separator), BF16),) * 2,
                [SM] + [VM] * 2,
                [pltpu.VMEM((separator, separator), F32)],
                moved=8 * separator * separator,
            )(mine_id, mine, other)
            matrices = [pltpu.with_memory_space_constraint(m, pltpu.HBM) for m in (inv, cpl)]
            outs += [shaped(inv.shape, BF16)] * 2 + [shaped(cpl.shape, BF16)] * 2
            outs += [shaped(cpl.shape[::-1], BF16)] * 2
            scratch += [
                pltpu.VMEM((2 * leaves, order // 2, order), F32),
                pltpu.VMEM((2 * leaves, order // 2, separator), F32),
                pltpu.SemaphoreType.DMA((2 * leaves,)),
                pltpu.SemaphoreType.DMA((2 * leaves,)),
            ]
        else:
            matrices = [inv_hi, inv_lo, cpl_t_hi, cpl_t_lo, cpl_hi, cpl_lo, sch_hi, sch_lo]
            scratch += [pltpu.VMEM((separator, loads), F32)]
        solution, dense, part, *made = call(
            functools.partial(leaf_kernel, width, first, last),
            "leaves",
            tuple(outs),
            [SM] * 4 + [VM] * (len(operands) - 4) + [HB if first else VM] * len(matrices),
            scratch,
            limit=24 if first else 12,
            flops=8 * leaves * order * loads * (order + 2 * separator),
            moved=16 * MIB,
        )(*operands, *matrices)
        if first:
            inv_hi, inv_lo, cpl_hi, cpl_lo, cpl_t_hi, cpl_t_lo = made

        def surface(pick, matrix):
            half = (rows // 2, columns)
            payload = shaped((chips, width + share, loads))
            scratch = [pltpu.VMEM((columns, 2 * loads), BF16)]
            if first:
                scratch += [
                    pltpu.VMEM((2, rows // 4, columns), F32),
                    pltpu.SemaphoreType.DMA((2, chips // 2)),
                ]
            return call(
                functools.partial(surface_kernel, width, first),
                "surface",
                (payload, shaped(half, BF16), shaped(half, BF16)) if first else (payload,),
                [SM] * 2 + [HB if first else VM] * len(matrix) + [VM] * (2 + len(pieces)),
                scratch,
                limit=14 if first else 8,
                flops=4 * rows * columns * loads,
                moved=6 * MIB,
            )(pick, group, *matrix, *pieces, dense, part)

        if first:
            bem_other, bem_mine = [bem_tiles], [bem_tiles]
        away, *made_other = surface(other_id, bem_other)
        swapped = lax.ppermute(away, "sub", swap)
        stay, *made_mine = surface(mine_id, bem_mine)
        payload = stay + swapped
        if first:
            bem_other, bem_mine = made_other, made_mine
            payload, sch_hi, sch_lo = lax.optimization_barrier((payload, sch_hi, sch_lo))
        got = over_chips(payload)
        if not last:
            field = call(
                functools.partial(field_kernel, width), "field", shaped((width, loads)), [VM] * 2,
                moved=MIB,
            )(got, surf_load)
            wide = call(
                functools.partial(wide_kernel, width),
                "wide",
                shaped((chips, width + share, loads)),
                [VM] * 2,
                moved=2 * MIB,
            )(got, field)
    pressure, sep_rows = call(
        functools.partial(final_kernel, width),
        "final",
        (shaped((width, loads)), shaped((share, loads))),
        [VM] * 2,
        moved=MIB,
    )(got, surf_load)
    return (solution[None], sep_rows[None], pressure)


def solution(mesh):
    return jax.shard_map(
        on_device,
        mesh=mesh,
        in_specs=(
            P("grp", "sub"),
            P("grp", "sub", None, None),
            P("grp", "sub", None, None),
            P("grp", None, "sub"),
            P("grp", "sub", None, None),
            P("grp", None, None),
            P(("grp", "sub"), None),
            P(("grp", "sub"), None),
            P("grp", "sub", None, None),
            P("grp", "sub", None, None),
            P("grp", "sub"),
            P("grp", "sub"),
            P("grp", "sub", None, None),
        ),
        out_specs=(P("grp", "sub", None, None), P("grp", "sub", None), P(("grp", "sub"), None)),
        check_vma=False,
    )
```

```python
import functools

import jax
import jax.numpy as jnp
from jax import lax
from jax.experimental import pallas as pl
from jax.experimental.pallas import tpu as pltpu
from jax.sharding import PartitionSpec as P

SWEEPS = 3
F32, BF16 = jnp.float32, jnp.bfloat16
VM = pl.BlockSpec(memory_space=pltpu.VMEM)
SM = pl.BlockSpec(memory_space=pltpu.SMEM)
HB = pl.BlockSpec(memory_space=pltpu.HBM)
MIB = 2**20


FIRST_STEP = 4
NEXT_STEPS = (1, 3, 2)


def origins():
    return [origin for step in (0, *NEXT_STEPS) for origin in (step, step ^ FIRST_STEP)]


def call(body, name, out, ins, scratch=(), limit=6, flops=0, moved=0):
    return pl.pallas_call(
        body,
        out_shape=out,
        in_specs=ins,
        out_specs=jax.tree.map(lambda _: VM, out),
        scratch_shapes=list(scratch),
        compiler_params=pltpu.CompilerParams(vmem_limit_bytes=limit * MIB),
        cost_estimate=pl.CostEstimate(flops=flops, bytes_accessed=moved, transcendentals=0),
        name=name,
    )


def shaped(shape, dtype=F32):
    return jax.ShapeDtypeStruct(shape, dtype)


def parted(x):
    hi = x.astype(BF16)
    return hi, (x - hi.astype(F32)).astype(BF16)


def widened(x):
    return jnp.concatenate(parted(x), axis=1)


def dot(a, b):
    return jnp.dot(a, b, preferred_element_type=F32)


def product(hi, lo, wide):
    n = wide.shape[1] // 2
    both = dot(hi, wide)
    return both[:, :n] + both[:, n:] + dot(lo, wide[:, :n])


def start_kernel(width, field, schur_t, wide, field_buf, schur_buf, sems):
    share, columns = schur_t.shape
    copies = [
        pltpu.make_async_copy(field, field_buf, sems.at[0]),
        pltpu.make_async_copy(schur_t, schur_buf, sems.at[1]),
    ]
    for copy in copies:
        copy.start()
    for copy in copies:
        copy.wait()
    for chip in range(wide.shape[0]):
        wide[chip, :width] = field_buf[...]
        for q in range(columns // width):
            rows = slice(width + q * share, width + (q + 1) * share)
            wide[chip, rows] = schur_buf[:, q * width : (q + 1) * width]


def turn_kernel(width, core_ref, mine, other, hi_ref, lo_ref, whole):
    chips = mine.shape[0]
    columns = whole.shape[1]
    share = whole.shape[0] // (2 * chips)
    core = core_ref[0]
    for chip in range(chips):
        at = 2 * chip * share
        for q in range(columns // width):
            rows = slice(width + q * share, width + (q + 1) * share)
            to = slice(q * width, (q + 1) * width)
            a, b = mine[chip, rows], other[chip, rows]
            whole[at : at + share, to] = jnp.where(core == 0, a, b)
            whole[at + share : at + 2 * share, to] = jnp.where(core == 0, b, a)
    hi_ref[...], lo_ref[...] = parted(whole[...].T)


def leaf_kernel(
    width, first, last,
    here_ref, owner_ref, size_ref, count_ref,
    load, flux_weight, trace_weight, sep_load, mine, other, *rest,
):
    if first:
        inv, cpl, dense, part, *rest = rest
        inv_hi, inv_lo, cpl_hi, cpl_lo, cpl_t_hi, cpl_t_lo, *rest = rest
        wide, wide_sol, inv_buf, cpl_buf, inv_sems, cpl_sems = rest
    else:
        inv_hi, inv_lo, cpl_t_hi, cpl_t_lo, cpl_hi, cpl_lo, sch_hi, sch_lo, *rest = rest
        *sol, dense, part, wide, wide_sol, gathered = rest
    leaves, order, loads = load.shape
    blocks = order // width
    chips = dense.shape[1]
    share = part.shape[0] // (2 * chips)
    here = here_ref[0]
    core = here % 2
    flux_t, trace_t = flux_weight[...].T, trace_weight[...].T
    half = order // 2
    cuts = [half // 2, half, order] if first else [order]

    def tiles(src, buf, sems, ends):
        return {
            end: pltpu.make_async_copy(src.at[pl.ds(start, end - start)], buf.at[pl.ds(start, end - start)], sems.at[i])
            for i, (start, end) in enumerate(zip([0, *ends], ends))
        }

    if first:
        inv_ends = [j * order + cut for j in range(leaves) for cut in cuts]
        cpl_ends = [(i + 1) * half for i in range(2 * leaves)]
        inv_copies = tiles(inv, inv_buf, inv_sems, inv_ends)
        cpl_copies = tiles(cpl, cpl_buf, cpl_sems, cpl_ends)
        for copy in [*inv_copies.values(), *cpl_copies.values()]:
            copy.start()

    def scale(turned, j, k):
        e = j * blocks + k
        return jnp.where(k < count_ref[0, j], turned[:, e : e + 1], 0.0)

    def live(j, k, x):
        row = k * width + lax.broadcasted_iota(jnp.int32, (width, loads), 0)
        return jnp.where(row < size_ref[0, j], x, 0.0)

    def surface(o):
        chip = o // 2
        return jnp.where(o - 2 * chip == core, mine[chip, :width], other[chip, :width])

    if not first:
        for chip in range(chips):
            a, b = mine[chip, width:], other[chip, width:]
            at = 2 * chip * share
            gathered[at : at + share] = jnp.where(core == 0, a, b)
            gathered[at + share : at + 2 * share] = jnp.where(core == 0, b, a)
        sep_wide = widened(product(sch_hi[...], sch_lo[...], widened(gathered[...])))
    dense[...] = jnp.zeros_like(dense)
    for j in range(leaves):
        if not first:
            rows = slice(j * order, (j + 1) * order)
            pulled = product(cpl_hi[rows], cpl_lo[rows], sep_wide)
        for k in range(blocks):
            at = slice(k * width, (k + 1) * width)
            rhs = load[j, at] - surface(owner_ref[0, j, 0, k]) * scale(flux_t, j, k)
            if not first:
                rhs = rhs - pulled[at]
            wide[j, at] = widened(live(j, k, rhs))
        for begin, end in zip([0, *cuts], cuts):
            start = j * order + begin
            rows = slice(start, j * order + end)
            if first:
                inv_copies[j * order + end].wait()
                hi, lo = parted(inv_buf[rows])
                inv_hi[rows], inv_lo[rows] = hi, lo
                got = product(hi, lo, wide[j])
            else:
                got = product(inv_hi[rows], inv_lo[rows], wide[j])
            for b in range((end - begin) // width):
                k = begin // width + b
                o = owner_ref[0, j, 0, k]
                chip = o // 2
                block = live(j, k, got[b * width : (b + 1) * width])
                if last:
                    sol[0][j, k * width : (k + 1) * width] = block
                dense[o - 2 * chip, chip] += block * scale(trace_t, j, k)
                at = slice(start + b * width, start + (b + 1) * width)
                wide_sol[at] = widened(block)
    left = jnp.where(here == 0, sep_load[...], 0.0)
    if first:
        for end, copy in cpl_copies.items():
            copy.wait()
            rows = slice(end - half, end)
            cpl_hi[rows], cpl_lo[rows] = parted(cpl_buf[rows])
            hi, lo = parted(cpl_buf[rows].T)
            cpl_t_hi[:, rows], cpl_t_lo[:, rows] = hi, lo
            left = left - product(hi, lo, wide_sol[rows])
    else:
        left = left - product(cpl_t_hi[...], cpl_t_lo[...], wide_sol[...])
    if last:
        left = product(sch_hi[...], sch_lo[...], widened(left))
    part[...] = left


def surface_kernel(width, first, pick_ref, group_ref, *rest):
    if first:
        src, *rest, out, hi_ref, lo_ref, wide, buf, sems = rest
    else:
        hi_ref, lo_ref, *rest, out, wide = rest
    *pieces, dense, part = rest
    pick = pick_ref[0]
    chips = out.shape[0]
    share = part.shape[0] // (2 * chips)
    parts = buf.shape[0] if first else 1
    tile = chips * width // parts

    def copies(i):
        found = []
        for b in range(tile // width):
            at = pl.multiple_of((2 * (i * (tile // width) + b) + pick) * width, width)
            found.append(
                pltpu.make_async_copy(
                    src.at[pl.ds(at, width)], buf.at[i, pl.ds(b * width, width)], sems.at[i, b]
                )
            )
        return found

    if first:
        flying = [copies(i) for i in range(parts)]
        for group in flying:
            for copy in group:
                copy.start()
    block = 0
    for piece in pieces:
        for i in range(piece.shape[0] // width):
            at = pl.multiple_of((group_ref[0] ^ origins()[block]) * width, width)
            wide[pl.ds(at, width)] = widened(piece[i * width : (i + 1) * width])
            block += 1
    for i in range(parts):
        rows = slice(i * tile, (i + 1) * tile)
        if first:
            for copy in flying[i]:
                copy.wait()
            hi, lo = parted(buf[i])
            hi_ref[rows], lo_ref[rows] = hi, lo
            got = product(hi, lo, wide[...])
        else:
            got = product(hi_ref[rows], lo_ref[rows], wide[...])
        for b in range(tile // width):
            chip = i * (tile // width) + b
            out[chip, :width] = dense[pick, chip] + got[b * width : (b + 1) * width]
            at = pl.multiple_of((2 * chip + pick) * share, share)
            out[chip, width:] = part[pl.ds(at, share)]


def summed(got, rows):
    total = got[0, rows]
    for chip in range(1, got.shape[0]):
        total = total + got[chip, rows]
    return total


def field_kernel(width, got, load, field):
    field[...] = load[...] + summed(got, slice(0, width))


def wide_kernel(width, got, field, wide):
    rest = summed(got, slice(width, None))
    for chip in range(wide.shape[0]):
        wide[chip, :width] = field[...]
        wide[chip, width:] = rest


def final_kernel(width, got, load, field, separator):
    field[...] = load[...] + summed(got, slice(0, width))
    separator[...] = summed(got, slice(width, None))


def on_device(
    bem_tiles,
    leaf_inverse,
    coupling,
    schur_inverse,
    leaf_load,
    sep_load,
    surf_load,
    surf_start,
    flux_weight,
    trace_weight,
    leaf_sizes,
    block_counts,
    block_owner,
):
    parts = lax.axis_size("sub")
    groups = lax.axis_size("grp")
    here = lax.axis_index("sub")
    core = lax.rem(here, 2).astype(jnp.int32)
    mine_id, other_id = core.reshape(1), (1 - core).reshape(1)
    here_id = here.astype(jnp.int32).reshape(1)
    group = lax.axis_index("grp").astype(jnp.int32).reshape(1)
    chips = parts // 2
    width, loads = surf_load.shape
    leaves, order = leaf_inverse.shape[1:3]
    blocks = order // width
    entries = leaves * blocks
    separator = schur_inverse.shape[1]
    share = schur_inverse.shape[2]
    rows = bem_tiles.shape[0]
    columns = bem_tiles.shape[1]
    same_core = [[2 * c + k for c in range(chips)] for k in range(2)]
    swap = [(i, i ^ 1) for i in range(parts)]

    def over_chips(x):
        return lax.all_to_all(x, "sub", 0, 0, axis_index_groups=same_core, tiled=True)

    def exchanged(x, step):
        return lax.ppermute(x, "grp", [(i, i ^ step) for i in range(groups)])

    inv = leaf_inverse.reshape(leaves * order, order)
    cpl = coupling.reshape(leaves * order, separator)
    field = surf_start
    wide = call(
        functools.partial(start_kernel, width),
        "start",
        shaped((chips, 2 * width, loads)),
        [HB] * 2,
        [
            pltpu.VMEM((width, loads), F32),
            pltpu.VMEM((share, separator), F32),
            pltpu.SemaphoreType.DMA((2,)),
        ],
        moved=MIB,
    )(*(pltpu.with_memory_space_constraint(x, pltpu.HBM) for x in (surf_start, schur_inverse[0].T)))
    wide, here_id, mine_id, other_id, group, owner = lax.optimization_barrier(
        (wide, here_id, mine_id, other_id, group, block_owner.transpose(0, 1, 3, 2))
    )
    for sweep in range(SWEEPS):
        first, last = sweep == 0, sweep == SWEEPS - 1
        beyond = exchanged(field, FIRST_STEP)
        wide, beyond = lax.optimization_barrier((wide, beyond))
        mine = over_chips(wide)
        mine, field, beyond = lax.optimization_barrier((mine, field, beyond))
        pair = jnp.concatenate([field, beyond], axis=0)
        pieces = [pair] + [exchanged(pair, step) for step in NEXT_STEPS]
        other = lax.ppermute(mine, "sub", swap)
        operands = [here_id, owner, leaf_sizes, block_counts, leaf_load[0]]
        operands += [w.reshape(entries, width) for w in (flux_weight, trace_weight)]
        operands += [sep_load[0], mine, other]
        outs = [shaped((leaves, order, loads))] if last else []
        outs += [
            shaped((2, chips, width, loads)),
            shaped((separator, loads)),
        ]
        scratch = [
            pltpu.VMEM((leaves, order, 2 * loads), BF16),
            pltpu.VMEM((leaves * order, 2 * loads), BF16),
        ]
        if first:
            sch_hi, sch_lo = call(
                functools.partial(turn_kernel, width),
                "split_schur",
                (shaped((separator, separator), BF16),) * 2,
                [SM] + [VM] * 2,
                [pltpu.VMEM((separator, separator), F32)],
                moved=8 * separator * separator,
            )(mine_id, mine, other)
            matrices = [pltpu.with_memory_space_constraint(m, pltpu.HBM) for m in (inv, cpl)]
            outs += [shaped(inv.shape, BF16)] * 2 + [shaped(cpl.shape, BF16)] * 2
            outs += [shaped(cpl.shape[::-1], BF16)] * 2
            scratch += [
                pltpu.VMEM(inv.shape, F32),
                pltpu.VMEM(cpl.shape, F32),
                pltpu.SemaphoreType.DMA((3 * leaves,)),
                pltpu.SemaphoreType.DMA((2 * leaves,)),
            ]
        else:
            matrices = [inv_hi, inv_lo, cpl_t_hi, cpl_t_lo, cpl_hi, cpl_lo, sch_hi, sch_lo]
            scratch += [pltpu.VMEM((separator, loads), F32)]
        made = call(
            functools.partial(leaf_kernel, width, first, last),
            "leaves",
            tuple(outs),
            [SM] * 4 + [VM] * (len(operands) - 4) + [HB if first else VM] * len(matrices),
            scratch,
            limit=24 if first else 12,
            flops=8 * leaves * order * loads * (order + 2 * separator),
            moved=16 * MIB,
        )(*operands, *matrices)
        if first:
            dense, part, inv_hi, inv_lo, cpl_hi, cpl_lo, cpl_t_hi, cpl_t_lo = made
        else:
            *solution, dense, part = made

        def surface(pick, matrix):
            half = (rows // 2, columns)
            payload = shaped((chips, width + share, loads))
            scratch = [pltpu.VMEM((columns, 2 * loads), BF16)]
            if first:
                scratch += [
                    pltpu.VMEM((2, rows // 4, columns), F32),
                    pltpu.SemaphoreType.DMA((2, chips // 2)),
                ]
            return call(
                functools.partial(surface_kernel, width, first),
                "surface",
                (payload, shaped(half, BF16), shaped(half, BF16)) if first else (payload,),
                [SM] * 2 + [HB if first else VM] * len(matrix) + [VM] * (2 + len(pieces)),
                scratch,
                limit=14 if first else 8,
                flops=4 * rows * columns * loads,
                moved=6 * MIB,
            )(pick, group, *matrix, *pieces, dense, part)

        if first:
            bem_other, bem_mine = [bem_tiles], [bem_tiles]
        away, *made_other = surface(other_id, bem_other)
        swapped = lax.ppermute(away, "sub", swap)
        stay, *made_mine = surface(mine_id, bem_mine)
        payload = stay + swapped
        if first:
            bem_other, bem_mine = made_other, made_mine
            payload, sch_hi, sch_lo = lax.optimization_barrier((payload, sch_hi, sch_lo))
        got = over_chips(payload)
        if not last:
            field = call(
                functools.partial(field_kernel, width), "field", shaped((width, loads)), [VM] * 2,
                moved=MIB,
            )(got, surf_load)
            wide = call(
                functools.partial(wide_kernel, width),
                "wide",
                shaped((chips, width + share, loads)),
                [VM] * 2,
                moved=2 * MIB,
            )(got, field)
    pressure, sep_rows = call(
        functools.partial(final_kernel, width),
        "final",
        (shaped((width, loads)), shaped((share, loads))),
        [VM] * 2,
        moved=MIB,
    )(got, surf_load)
    return (solution[0][None], sep_rows[None], pressure)


def solution(mesh):
    return jax.shard_map(
        on_device,
        mesh=mesh,
        in_specs=(
            P("grp", "sub"),
            P("grp", "sub", None, None),
            P("grp", "sub", None, None),
            P("grp", None, "sub"),
            P("grp", "sub", None, None),
            P("grp", None, None),
            P(("grp", "sub"), None),
            P(("grp", "sub"), None),
            P("grp", "sub", None, None),
            P("grp", "sub", None, None),
            P("grp", "sub"),
            P("grp", "sub"),
            P("grp", "sub", None, None),
        ),
        out_specs=(P("grp", "sub", None, None), P("grp", "sub", None), P(("grp", "sub"), None)),
        check_vma=False,
    )
```

```python
import functools

import jax
import jax.numpy as jnp
from jax import lax
from jax.experimental import pallas as pl
from jax.experimental.pallas import tpu as pltpu
from jax.sharding import PartitionSpec as P

SWEEPS = 3
F32, BF16 = jnp.float32, jnp.bfloat16
VM = pl.BlockSpec(memory_space=pltpu.VMEM)
SM = pl.BlockSpec(memory_space=pltpu.SMEM)
HB = pl.BlockSpec(memory_space=pltpu.HBM)
MIB = 2**20


FIRST_STEP = 4
NEXT_STEPS = (1, 3, 2)


def origins():
    return [origin for step in (0, *NEXT_STEPS) for origin in (step, step ^ FIRST_STEP)]


def call(body, name, out, ins, scratch=(), limit=6, flops=0, moved=0):
    return pl.pallas_call(
        body,
        out_shape=out,
        in_specs=ins,
        out_specs=jax.tree.map(lambda _: VM, out),
        scratch_shapes=list(scratch),
        compiler_params=pltpu.CompilerParams(vmem_limit_bytes=limit * MIB),
        cost_estimate=pl.CostEstimate(flops=flops, bytes_accessed=moved, transcendentals=0),
        name=name,
    )


def shaped(shape, dtype=F32):
    return jax.ShapeDtypeStruct(shape, dtype)


def parted(x):
    hi = x.astype(BF16)
    return hi, (x - hi.astype(F32)).astype(BF16)


def widened(x):
    return jnp.concatenate(parted(x), axis=1)


def dot(a, b):
    return jnp.dot(a, b, preferred_element_type=F32)


def product(hi, lo, wide):
    n = wide.shape[1] // 2
    both = dot(hi, wide)
    return both[:, :n] + both[:, n:] + dot(lo, wide[:, :n])


def start_kernel(width, field, schur_t, wide, field_buf, schur_buf, sems):
    share, columns = schur_t.shape
    copies = [
        pltpu.make_async_copy(field, field_buf, sems.at[0]),
        pltpu.make_async_copy(schur_t, schur_buf, sems.at[1]),
    ]
    for copy in copies:
        copy.start()
    for copy in copies:
        copy.wait()
    for chip in range(wide.shape[0]):
        wide[chip, :width] = field_buf[...]
        for q in range(columns // width):
            rows = slice(width + q * share, width + (q + 1) * share)
            wide[chip, rows] = schur_buf[:, q * width : (q + 1) * width]


def turn_kernel(width, core_ref, mine, other, hi_ref, lo_ref, whole):
    chips = mine.shape[0]
    columns = whole.shape[1]
    share = whole.shape[0] // (2 * chips)
    core = core_ref[0]
    for chip in range(chips):
        at = 2 * chip * share
        for q in range(columns // width):
            rows = slice(width + q * share, width + (q + 1) * share)
            to = slice(q * width, (q + 1) * width)
            a, b = mine[chip, rows], other[chip, rows]
            whole[at : at + share, to] = jnp.where(core == 0, a, b)
            whole[at + share : at + 2 * share, to] = jnp.where(core == 0, b, a)
    hi_ref[...], lo_ref[...] = parted(whole[...].T)


def leaf_kernel(
    width, first, last,
    here_ref, owner_ref, size_ref, count_ref,
    load, flux_weight, trace_weight, sep_load, mine, other, *rest,
):
    if first:
        inv, cpl, dense, part, *rest = rest
        inv_hi, inv_lo, cpl_hi, cpl_lo, cpl_t_hi, cpl_t_lo, *rest = rest
        wide, wide_sol, inv_buf, cpl_buf, inv_sems, cpl_sems = rest
    else:
        inv_hi, inv_lo, cpl_t_hi, cpl_t_lo, cpl_hi, cpl_lo, sch_hi, sch_lo, *rest = rest
        *sol, dense, part, wide, wide_sol, gathered = rest
    leaves, order, loads = load.shape
    blocks = order // width
    chips = dense.shape[1]
    share = part.shape[0] // (2 * chips)
    here = here_ref[0]
    core = here % 2
    flux_t, trace_t = flux_weight[...].T, trace_weight[...].T
    half = order // 2
    cuts = [half // 2, half, order] if first else [order]

    def tiles(src, buf, sems, ends):
        return {
            end: pltpu.make_async_copy(src.at[pl.ds(start, end - start)], buf.at[pl.ds(start, end - start)], sems.at[i])
            for i, (start, end) in enumerate(zip([0, *ends], ends))
        }

    if first:
        inv_ends = [j * order + cut for j in range(leaves) for cut in cuts]
        cpl_ends = [(i + 1) * half for i in range(2 * leaves)]
        inv_copies = tiles(inv, inv_buf, inv_sems, inv_ends)
        cpl_copies = tiles(cpl, cpl_buf, cpl_sems, cpl_ends)
        for copy in [*inv_copies.values(), *cpl_copies.values()]:
            copy.start()

    def scale(turned, j, k):
        e = j * blocks + k
        return jnp.where(k < count_ref[0, j], turned[:, e : e + 1], 0.0)

    def live(j, k, x):
        row = k * width + lax.broadcasted_iota(jnp.int32, (width, loads), 0)
        return jnp.where(row < size_ref[0, j], x, 0.0)

    def surface(o):
        chip = o // 2
        return jnp.where(o - 2 * chip == core, mine[chip, :width], other[chip, :width])

    if not first:
        for chip in range(chips):
            a, b = mine[chip, width:], other[chip, width:]
            at = 2 * chip * share
            gathered[at : at + share] = jnp.where(core == 0, a, b)
            gathered[at + share : at + 2 * share] = jnp.where(core == 0, b, a)
        sep_wide = widened(product(sch_hi[...], sch_lo[...], widened(gathered[...])))
    dense[...] = jnp.zeros_like(dense)
    for j in range(leaves):
        if not first:
            rows = slice(j * order, (j + 1) * order)
            pulled = product(cpl_hi[rows], cpl_lo[rows], sep_wide)
        for k in range(blocks):
            at = slice(k * width, (k + 1) * width)
            rhs = load[j, at] - surface(owner_ref[0, j, 0, k]) * scale(flux_t, j, k)
            if not first:
                rhs = rhs - pulled[at]
            wide[j, at] = widened(live(j, k, rhs))
        for begin, end in zip([0, *cuts], cuts):
            start = j * order + begin
            rows = slice(start, j * order + end)
            if first:
                inv_copies[j * order + end].wait()
                hi, lo = parted(inv_buf[rows])
                inv_hi[rows], inv_lo[rows] = hi, lo
                got = product(hi, lo, wide[j])
            else:
                got = product(inv_hi[rows], inv_lo[rows], wide[j])
            for b in range((end - begin) // width):
                k = begin // width + b
                o = owner_ref[0, j, 0, k]
                chip = o // 2
                block = live(j, k, got[b * width : (b + 1) * width])
                if last:
                    sol[0][j, k * width : (k + 1) * width] = block
                dense[o - 2 * chip, chip] += block * scale(trace_t, j, k)
                at = slice(start + b * width, start + (b + 1) * width)
                wide_sol[at] = widened(block)
    left = jnp.where(here == 0, sep_load[...], 0.0)
    if first:
        for end, copy in cpl_copies.items():
            copy.wait()
            rows = slice(end - half, end)
            cpl_hi[rows], cpl_lo[rows] = parted(cpl_buf[rows])
            hi, lo = parted(cpl_buf[rows].T)
            cpl_t_hi[:, rows], cpl_t_lo[:, rows] = hi, lo
            left = left - product(hi, lo, wide_sol[rows])
    else:
        left = left - product(cpl_t_hi[...], cpl_t_lo[...], wide_sol[...])
    if last:
        left = product(sch_hi[...], sch_lo[...], widened(left))
    part[...] = left


def surface_kernel(width, first, made, pick_ref, group_ref, *rest):
    if first:
        src, *rest, buf, sems = rest
    else:
        hi_ref, lo_ref, *rest = rest
    if made:
        wide, dense, part, out, *rest = rest
        pieces = []
    else:
        *pieces, dense, part, out, wide = rest[:-2] if first else rest
        rest = rest[-2:]
    if first:
        hi_ref, lo_ref = rest
    pick = pick_ref[0]
    chips = out.shape[0]
    share = part.shape[0] // (2 * chips)
    parts = buf.shape[0] if first else 1
    tile = chips * width // parts

    def copies(i):
        found = []
        for b in range(tile // width):
            at = pl.multiple_of((2 * (i * (tile // width) + b) + pick) * width, width)
            found.append(
                pltpu.make_async_copy(
                    src.at[pl.ds(at, width)], buf.at[i, pl.ds(b * width, width)], sems.at[i, b]
                )
            )
        return found

    if first:
        flying = [copies(i) for i in range(parts)]
        for group in flying:
            for copy in group:
                copy.start()
    block = 0
    for piece in pieces:
        for i in range(piece.shape[0] // width):
            at = pl.multiple_of((group_ref[0] ^ origins()[block]) * width, width)
            wide[pl.ds(at, width)] = widened(piece[i * width : (i + 1) * width])
            block += 1
    for i in range(parts):
        rows = slice(i * tile, (i + 1) * tile)
        if first:
            for copy in flying[i]:
                copy.wait()
            hi, lo = parted(buf[i])
            hi_ref[rows], lo_ref[rows] = hi, lo
            got = product(hi, lo, wide[...])
        else:
            got = product(hi_ref[rows], lo_ref[rows], wide[...])
        for b in range(tile // width):
            chip = i * (tile // width) + b
            out[chip, :width] = dense[pick, chip] + got[b * width : (b + 1) * width]
            at = pl.multiple_of((2 * chip + pick) * share, share)
            out[chip, width:] = part[pl.ds(at, share)]


def summed(got, rows):
    total = got[0, rows]
    for chip in range(1, got.shape[0]):
        total = total + got[chip, rows]
    return total


def field_kernel(width, got, load, field):
    field[...] = load[...] + summed(got, slice(0, width))


def wide_kernel(width, got, field, wide):
    rest = summed(got, slice(width, None))
    for chip in range(wide.shape[0]):
        wide[chip, :width] = field[...]
        wide[chip, width:] = rest


def final_kernel(width, got, load, field, separator):
    field[...] = load[...] + summed(got, slice(0, width))
    separator[...] = summed(got, slice(width, None))


def on_device(
    bem_tiles,
    leaf_inverse,
    coupling,
    schur_inverse,
    leaf_load,
    sep_load,
    surf_load,
    surf_start,
    flux_weight,
    trace_weight,
    leaf_sizes,
    block_counts,
    block_owner,
):
    parts = lax.axis_size("sub")
    groups = lax.axis_size("grp")
    here = lax.axis_index("sub")
    core = lax.rem(here, 2).astype(jnp.int32)
    mine_id, other_id = core.reshape(1), (1 - core).reshape(1)
    here_id = here.astype(jnp.int32).reshape(1)
    group = lax.axis_index("grp").astype(jnp.int32).reshape(1)
    chips = parts // 2
    width, loads = surf_load.shape
    leaves, order = leaf_inverse.shape[1:3]
    blocks = order // width
    entries = leaves * blocks
    separator = schur_inverse.shape[1]
    share = schur_inverse.shape[2]
    rows = bem_tiles.shape[0]
    columns = bem_tiles.shape[1]
    same_core = [[2 * c + k for c in range(chips)] for k in range(2)]
    swap = [(i, i ^ 1) for i in range(parts)]

    def over_chips(x):
        return lax.all_to_all(x, "sub", 0, 0, axis_index_groups=same_core, tiled=True)

    def exchanged(x, step):
        return lax.ppermute(x, "grp", [(i, i ^ step) for i in range(groups)])

    inv = leaf_inverse.reshape(leaves * order, order)
    cpl = coupling.reshape(leaves * order, separator)
    field = surf_start
    wide = call(
        functools.partial(start_kernel, width),
        "start",
        shaped((chips, 2 * width, loads)),
        [HB] * 2,
        [
            pltpu.VMEM((width, loads), F32),
            pltpu.VMEM((share, separator), F32),
            pltpu.SemaphoreType.DMA((2,)),
        ],
        moved=MIB,
    )(*(pltpu.with_memory_space_constraint(x, pltpu.HBM) for x in (surf_start, schur_inverse[0].T)))
    wide, here_id, mine_id, other_id, group, owner = lax.optimization_barrier(
        (wide, here_id, mine_id, other_id, group, block_owner.transpose(0, 1, 3, 2))
    )
    for sweep in range(SWEEPS):
        first, last = sweep == 0, sweep == SWEEPS - 1
        beyond = exchanged(field, FIRST_STEP)
        wide, beyond = lax.optimization_barrier((wide, beyond))
        mine = over_chips(wide)
        mine, field, beyond = lax.optimization_barrier((mine, field, beyond))
        pair = jnp.concatenate([field, beyond], axis=0)
        pieces = [pair] + [exchanged(pair, step) for step in NEXT_STEPS]
        other = lax.ppermute(mine, "sub", swap)
        operands = [here_id, owner, leaf_sizes, block_counts, leaf_load[0]]
        operands += [w.reshape(entries, width) for w in (flux_weight, trace_weight)]
        operands += [sep_load[0], mine, other]
        outs = [shaped((leaves, order, loads))] if last else []
        outs += [
            shaped((2, chips, width, loads)),
            shaped((separator, loads)),
        ]
        scratch = [
            pltpu.VMEM((leaves, order, 2 * loads), BF16),
            pltpu.VMEM((leaves * order, 2 * loads), BF16),
        ]
        if first:
            sch_hi, sch_lo = call(
                functools.partial(turn_kernel, width),
                "split_schur",
                (shaped((separator, separator), BF16),) * 2,
                [SM] + [VM] * 2,
                [pltpu.VMEM((separator, separator), F32)],
                moved=8 * separator * separator,
            )(mine_id, mine, other)
            matrices = [pltpu.with_memory_space_constraint(m, pltpu.HBM) for m in (inv, cpl)]
            outs += [shaped(inv.shape, BF16)] * 2 + [shaped(cpl.shape, BF16)] * 2
            outs += [shaped(cpl.shape[::-1], BF16)] * 2
            scratch += [
                pltpu.VMEM(inv.shape, F32),
                pltpu.VMEM(cpl.shape, F32),
                pltpu.SemaphoreType.DMA((3 * leaves,)),
                pltpu.SemaphoreType.DMA((2 * leaves,)),
            ]
        else:
            matrices = [inv_hi, inv_lo, cpl_t_hi, cpl_t_lo, cpl_hi, cpl_lo, sch_hi, sch_lo]
            scratch += [pltpu.VMEM((separator, loads), F32)]
        made = call(
            functools.partial(leaf_kernel, width, first, last),
            "leaves",
            tuple(outs),
            [SM] * 4 + [VM] * (len(operands) - 4) + [HB if first else VM] * len(matrices),
            scratch,
            limit=24 if first else 12,
            flops=8 * leaves * order * loads * (order + 2 * separator),
            moved=16 * MIB,
        )(*operands, *matrices)
        if first:
            dense, part, inv_hi, inv_lo, cpl_hi, cpl_lo, cpl_t_hi, cpl_t_lo = made
        else:
            *solution, dense, part = made

        def surface(pick, matrix, column, made):
            half = (rows // 2, columns)
            payload = shaped((chips, width + share, loads))
            scratch = []
            if first:
                scratch = [
                    pltpu.VMEM((2, rows // 4, columns), F32),
                    pltpu.SemaphoreType.DMA((2, chips // 2)),
                ]
            outs = [payload] + ([] if made else [shaped((columns, 2 * loads), BF16)])
            outs += [shaped(half, BF16)] * 2 if first else []
            return call(
                functools.partial(surface_kernel, width, first, made),
                "surface",
                tuple(outs),
                [SM] * 2 + [HB if first else VM] * len(matrix) + [VM] * (2 + len(column)),
                scratch,
                limit=14 if first else 8,
                flops=4 * rows * columns * loads,
                moved=6 * MIB,
            )(pick, group, *matrix, *column, dense, part)

        if first:
            bem_other, bem_mine = [bem_tiles], [bem_tiles]
        away, split_column, *made_other = surface(other_id, bem_other, pieces, False)
        swapped = lax.ppermute(away, "sub", swap)
        stay, *made_mine = surface(mine_id, bem_mine, [split_column], True)
        payload = stay + swapped
        if first:
            bem_other, bem_mine = made_other, made_mine
            payload, sch_hi, sch_lo = lax.optimization_barrier((payload, sch_hi, sch_lo))
        got = over_chips(payload)
        if not last:
            field = call(
                functools.partial(field_kernel, width), "field", shaped((width, loads)), [VM] * 2,
                moved=MIB,
            )(got, surf_load)
            wide = call(
                functools.partial(wide_kernel, width),
                "wide",
                shaped((chips, width + share, loads)),
                [VM] * 2,
                moved=2 * MIB,
            )(got, field)
    pressure, sep_rows = call(
        functools.partial(final_kernel, width),
        "final",
        (shaped((width, loads)), shaped((share, loads))),
        [VM] * 2,
        moved=MIB,
    )(got, surf_load)
    return (solution[0][None], sep_rows[None], pressure)


def solution(mesh):
    return jax.shard_map(
        on_device,
        mesh=mesh,
        in_specs=(
            P("grp", "sub"),
            P("grp", "sub", None, None),
            P("grp", "sub", None, None),
            P("grp", None, "sub"),
            P("grp", "sub", None, None),
            P("grp", None, None),
            P(("grp", "sub"), None),
            P(("grp", "sub"), None),
            P("grp", "sub", None, None),
            P("grp", "sub", None, None),
            P("grp", "sub"),
            P("grp", "sub"),
            P("grp", "sub", None, None),
        ),
        out_specs=(P("grp", "sub", None, None), P("grp", "sub", None), P(("grp", "sub"), None)),
        check_vma=False,
    )
```
